32 devices in a mesh: dp: 8 (over y, x, core), mp: 4 (over z).
Axes of the slice: x: 2, y: 2, z: 4, core: 2. Of those that a mesh axis runs over, the one named last changes fastest.
Arguments:
- inputs: bfloat16 [8192, 3072], P(('dp', 'mp')), may hold values from -64 to 64, as said below
- w_qkv: bfloat16 [3072, 3, 3072], P('dp', None, 'mp'), may hold values from -2 to 2
- w_out: bfloat16 [3072, 3072], P('mp', 'dp'), may hold values from -0.109375 to 0.109375
- upstream: bfloat16 [8192, 3072], P(('dp', 'mp')), may hold values from -6 to 6
Outputs:
- layer_out: bfloat16 [8192, 3072], P(('dp', 'mp'))
- grad_x: bfloat16 [8192, 3072], P(('dp', 'mp'))
- grad_wqkv: bfloat16 [3072, 3, 3072], P('dp', None, 'mp')
- grad_wout: bfloat16 [3072, 3072], P('mp', 'dp')
The draws below stay inside these ranges and needn't reach their ends.
Inputs may be any that keep to these rules, and one draw needn't show every extreme that they name: `inputs`: Activations; each row's scale may differ.
All inputs are finite; a program needn't handle non-finite values.
Results may differ from the reference program's by a relative error of at most 0.014.
The reference program's roundings to bfloat16 on the way (of `normed`, `projected`, `probs16`, `context`, `grad_context`, `grad_values`, `grad_scores` and `grad_projected`) count: a program that leaves them out, or rounds other values in their place, can miss the bound.
Values may be sent and summed in bfloat16 or wider, within the bound.
A program may use at most 128 MiB of HBM per device.

```python
import jax
import jax.numpy as jnp
from jax import lax

D = 3072
HEADS = 24
HD = 128
PATCH = 256
IMG_DEV = 4
A = 3072
TOKENS = 8192
N_DP = 8
N_MP = 4


def draw_inputs(key, part):
    first_key = jax.random.fold_in(key, 0)
    base = jnp.clip(jax.random.normal(first_key, (TOKENS, D), jnp.float32), -6.0, 6.0)
    return base.astype(jnp.bfloat16)


def draw_w_qkv(key, part):
    query_key, key_key, value_key = jax.random.split(key, 3)
    spread = D ** (-0.5)
    queries = jnp.clip(jax.random.normal(query_key, (D, 1, HEADS, HD), jnp.float32), -4.0, 4.0) * spread
    keys_part = jnp.clip(jax.random.normal(key_key, (D, 1, HEADS, HD), jnp.float32), -4.0, 4.0) * spread
    values_part = jnp.clip(jax.random.normal(value_key, (D, 1, HEADS, HD), jnp.float32), -4.0, 4.0) * spread
    return jnp.concatenate([queries, keys_part, values_part], axis=1).reshape(D, 3, HEADS * HD).astype(jnp.bfloat16)


def level_of(stream_key, shape, shards, smallest, largest):
    loudness, own = 1.0, jax.random.fold_in(stream_key, 6)
    for dim, parts in shards:
        steps = jnp.exp(jax.random.uniform(jax.random.fold_in(own, dim), (parts,), jnp.float32, smallest / len(shards), largest / len(shards)))
        loudness = loudness * jnp.repeat(steps, shape[dim] // parts).reshape([-1 if axis == dim else 1 for axis in range(len(shape))])
    return loudness


def scatter_about(own_key, extent, deviation, bound, cuts=(), dtype=jnp.bfloat16):
    gain = level_of(own_key, extent, cuts, -0.22, 0.18) if cuts else 1.0
    drawn = jax.random.normal(own_key, extent, jnp.float32) * deviation * gain
    return jnp.minimum(jnp.maximum(drawn, -bound), bound).astype(dtype)


def setup_inputs(seed: int = 0) -> dict:
    streams_of = jax.random.split(jax.random.key(seed), 5)
    inputs = draw_inputs(jax.random.fold_in(streams_of[4], 71), 0)
    w_qkv = draw_w_qkv(jax.random.fold_in(streams_of[4], 71), 0)
    w_out = scatter_about(streams_of[2], (A, D), A ** -0.5, 0.109375, ((0, 4), (1, 8)))
    upstream = scatter_about(streams_of[3], (TOKENS, D), 1.0, 6.0, ((0, 32),))
    return {"inputs": inputs, "w_qkv": w_qkv, "w_out": w_out, "upstream": upstream}


def rounded(values):
    return lax.optimization_barrier(values.astype(jnp.bfloat16)).astype(jnp.float32)

def reference(inputs, w_qkv, w_out, upstream):
    rows_group = IMG_DEV * PATCH
    local_width = A // N_MP
    inputs_float = inputs.astype(jnp.float32)
    centred = inputs_float - lax.optimization_barrier(jnp.mean(inputs_float, axis=1, keepdims=True))
    inv_scale = lax.rsqrt(lax.optimization_barrier(jnp.mean(centred * centred, axis=1, keepdims=True)) + 1e-06)
    standard = centred * inv_scale
    normed = standard.astype(jnp.bfloat16)
    projected = jnp.dot(normed, w_qkv.reshape(D, 3 * A), preferred_element_type=jnp.float32).astype(jnp.bfloat16)
    split_view = projected.reshape(TOKENS // PATCH, PATCH, 3, HEADS, HD)
    queries = split_view[:, :, 0].astype(jnp.float32)
    keys_part = split_view[:, :, 1].astype(jnp.float32)
    values_part = split_view[:, :, 2].astype(jnp.float32)
    scale = HD ** (-0.5)
    scores = jnp.einsum('bqhe,bkhe->bhqk', queries, keys_part) * scale
    probs = jax.nn.softmax(scores, axis=-1)
    probs16 = probs.astype(jnp.bfloat16)
    context = jnp.einsum('bhqk,bkhe->bqhe', probs16.astype(jnp.float32), values_part).astype(jnp.bfloat16).reshape(TOKENS, A)
    attended = jnp.zeros((TOKENS, D), jnp.float32)
    for shard in range(N_MP):
        low = shard * local_width
        attended = attended + rounded(jnp.dot(context[:, low:low + local_width], w_out[low:low + local_width], preferred_element_type=jnp.float32))
    layer_out = (inputs_float + attended).astype(jnp.bfloat16)
    grad_context = jnp.dot(upstream, w_out.T, preferred_element_type=jnp.float32).astype(jnp.bfloat16)
    grad_wout = jnp.zeros((A, D), jnp.float32)
    for group in range(N_DP):
        low = group * rows_group
        grad_wout = grad_wout + rounded(jnp.dot(context[low:low + rows_group].T, upstream[low:low + rows_group], preferred_element_type=jnp.float32))
    grad_heads = grad_context.reshape(TOKENS // PATCH, PATCH, HEADS, HD).astype(jnp.float32)
    grad_probs = jnp.einsum('bqhe,bkhe->bhqk', grad_heads, values_part)
    grad_values = jnp.einsum('bhqk,bqhe->bkhe', probs16.astype(jnp.float32), grad_heads).astype(jnp.bfloat16)
    row_totals = lax.optimization_barrier(jnp.sum(probs * grad_probs, axis=-1, keepdims=True))
    grad_scores = (probs * (grad_probs - row_totals) * scale).astype(jnp.bfloat16).astype(jnp.float32)
    grad_queries = jnp.einsum('bhqk,bkhe->bqhe', grad_scores, keys_part).astype(jnp.bfloat16)
    grad_keys = jnp.einsum('bhqk,bqhe->bkhe', grad_scores, queries).astype(jnp.bfloat16)
    grad_projected = jnp.stack([grad_queries, grad_keys, grad_values], axis=2).reshape(TOKENS, 3, A)
    grad_normed = jnp.zeros((TOKENS, D), jnp.float32)
    for shard in range(N_MP):
        low = shard * local_width
        piece = grad_projected[:, :, low:low + local_width].reshape(TOKENS, 3 * local_width)
        weight_piece = w_qkv[:, :, low:low + local_width].reshape(D, 3 * local_width)
        grad_normed = grad_normed + rounded(jnp.dot(piece, weight_piece.T, preferred_element_type=jnp.float32))
    centre_grad = lax.optimization_barrier(jnp.mean(grad_normed, axis=1, keepdims=True))
    along = lax.optimization_barrier(jnp.mean(grad_normed * standard, axis=1, keepdims=True))
    grad_x = (upstream.astype(jnp.float32) + inv_scale * (grad_normed - centre_grad - standard * along)).astype(jnp.bfloat16)
    flat_grad = grad_projected.reshape(TOKENS, 3 * A)
    grad_wqkv = jnp.zeros((D, 3 * A), jnp.float32)
    for group in range(N_DP):
        low = group * rows_group
        grad_wqkv = grad_wqkv + rounded(jnp.dot(normed[low:low + rows_group].T, flat_grad[low:low + rows_group], preferred_element_type=jnp.float32))
    grad_wqkv = grad_wqkv.reshape(D, 3, A).astype(jnp.bfloat16)
    return (layer_out, grad_x, grad_wqkv, grad_wout.astype(jnp.bfloat16))
```

```python
import functools

import jax
import jax.numpy as jnp
from jax import lax
from jax.experimental import pallas as pl
from jax.experimental.pallas import tpu as pltpu
from jax.sharding import PartitionSpec as P

HD = 128
PATCH = 256
SCALE = HD ** (-0.5)
epsilon = 1e-06
VMEM_BYTES = 32 * 1024 * 1024

NT = (((1,), (1,)), ((), ()))
TN = (((0,), (0,)), ((), ()))
NN = (((1,), (0,)), ((), ()))


def dot(left, right, dims):
    return lax.dot_general(left, right, dims, preferred_element_type=jnp.float32)


def softmax_of(queries, keys):
    scores = dot(queries, keys, NT) * SCALE
    weights = jnp.exp(scores - jnp.max(scores, axis=-1, keepdims=True))
    return weights / jnp.sum(weights, axis=-1, keepdims=True)


def forward_kernel(projected_ref, context_ref):
    width = context_ref.shape[1]
    for low in range(0, width, HD):
        queries = projected_ref[:, low:low + HD]
        keys = projected_ref[:, width + low:width + low + HD]
        values = projected_ref[:, 2 * width + low:2 * width + low + HD]
        probs16 = softmax_of(queries, keys).astype(jnp.bfloat16)
        context_ref[:, low:low + HD] = dot(probs16, values, NN).astype(jnp.bfloat16)


def backward_kernel(projected_ref, grad_context_ref, grad_ref):
    width = grad_context_ref.shape[1]
    for low in range(0, width, HD):
        queries = projected_ref[:, low:low + HD]
        keys = projected_ref[:, width + low:width + low + HD]
        values = projected_ref[:, 2 * width + low:2 * width + low + HD]
        grad_heads = grad_context_ref[:, low:low + HD]
        probs = softmax_of(queries, keys)
        probs16 = probs.astype(jnp.bfloat16)
        grad_probs = dot(grad_heads, values, NT)
        row_totals = jnp.sum(probs * grad_probs, axis=-1, keepdims=True)
        grad_scores = (probs * (grad_probs - row_totals) * SCALE).astype(jnp.bfloat16)
        grad_ref[:, low:low + HD] = dot(grad_scores, keys, NN).astype(jnp.bfloat16)
        grad_ref[:, width + low:width + low + HD] = dot(grad_scores, queries, TN).astype(jnp.bfloat16)
        grad_ref[:, 2 * width + low:2 * width + low + HD] = dot(probs16, grad_heads, TN).astype(
            jnp.bfloat16
        )


def rows_spec(columns):
    return pl.BlockSpec((PATCH, columns), lambda image: (image, 0))


def attention_forward(projected):
    rows, width = projected.shape[0], projected.shape[1] // 3
    pairs = rows * width * PATCH // HD
    return pl.pallas_call(
        forward_kernel,
        grid=(rows // PATCH,),
        in_specs=[rows_spec(3 * width)],
        out_specs=rows_spec(width),
        out_shape=jax.ShapeDtypeStruct((rows, width), jnp.bfloat16),
        compiler_params=pltpu.CompilerParams(vmem_limit_bytes=VMEM_BYTES),
        cost_estimate=pl.CostEstimate(
            flops=4 * pairs * HD, bytes_accessed=8 * rows * width, transcendentals=pairs
        ),
        name="attention_forward",
    )(projected)


def attention_backward(projected, grad_context):
    rows, width = grad_context.shape
    pairs = rows * width * PATCH // HD
    return pl.pallas_call(
        backward_kernel,
        grid=(rows // PATCH,),
        in_specs=[rows_spec(3 * width), rows_spec(width)],
        out_specs=rows_spec(3 * width),
        out_shape=jax.ShapeDtypeStruct((rows, 3 * width), jnp.bfloat16),
        compiler_params=pltpu.CompilerParams(vmem_limit_bytes=VMEM_BYTES),
        cost_estimate=pl.CostEstimate(
            flops=10 * pairs * HD, bytes_accessed=14 * rows * width, transcendentals=pairs
        ),
        name="attention_backward",
    )(projected, grad_context)


def line_gather(block, axis, count):
    me = lax.axis_index(axis)
    right, left = [block], [block]
    for step in range(1, count):
        right.append(
            lax.ppermute(right[-1], axis, [(i, i + 1) for i in range(step - 1, count - 1)])
        )
        left.append(lax.ppermute(left[-1], axis, [(i, i - 1) for i in range(1, count - step + 1)]))
    blocks = [block]
    for k in range(1, count):
        blocks.append(jnp.where(me >= k, right[k], left[count - k]))
    return blocks, (right[-1], left[-1])


def line_scatter_sum(parts, axis, count):
    from_left = from_right = None
    for step in range(1, count):
        rightward, leftward = parts[step], parts[count - step]
        if step > 1:
            rightward = (rightward.astype(jnp.float32) + from_left.astype(jnp.float32)).astype(
                jnp.bfloat16
            )
            leftward = (leftward.astype(jnp.float32) + from_right.astype(jnp.float32)).astype(
                jnp.bfloat16
            )
        from_left = lax.ppermute(
            rightward, axis, [(i, i + 1) for i in range(0, min(step, count - 1))]
        )
        from_right = lax.ppermute(
            leftward, axis, [(i, i - 1) for i in range(max(count - step, 1), count)]
        )
    total = parts[0].astype(jnp.float32)
    if from_left is not None:
        total = total + from_left.astype(jnp.float32) + from_right.astype(jnp.float32)
    return total


def per_device(count, inputs, w_qkv, w_out, upstream):
    local_rows, width = inputs.shape
    local_width = w_qkv.shape[2]
    inputs_float = inputs.astype(jnp.float32)
    centred = inputs_float - jnp.mean(inputs_float, axis=1, keepdims=True)
    inv_scale = lax.rsqrt(jnp.mean(centred * centred, axis=1, keepdims=True) + epsilon)
    standard = centred * inv_scale
    normed_local = standard.astype(jnp.bfloat16)

    qkv_matrix = lax.all_gather(w_qkv, "dp", axis=0, tiled=True).reshape(width, 3 * local_width)
    out_turned = lax.all_gather(w_out.T, "dp", axis=0, tiled=True)

    def turned(blocks):
        if local_rows % PATCH == 0:
            return blocks
        stacked, me = jnp.stack(blocks), lax.axis_index("mp")
        return [
            lax.dynamic_index_in_dim(stacked, lax.rem(me + count - k, count), keepdims=False)
            for k in range(count)
        ]

    normed_blocks, last = line_gather(normed_local, "mp", count)
    normed = jnp.concatenate(turned(normed_blocks), axis=0)
    upstream_later, _, _ = lax.optimization_barrier((upstream,) + last)
    cotangent_blocks, _ = line_gather(upstream_later, "mp", count)
    cotangent = jnp.concatenate(turned(cotangent_blocks), axis=0)

    def by_block(rows):
        return turned([rows[k * local_rows:(k + 1) * local_rows] for k in range(count)])

    projected = dot(normed, qkv_matrix, NN).astype(jnp.bfloat16)
    context = attention_forward(projected)
    attended_parts = dot(context, out_turned, NT).astype(jnp.bfloat16)
    attended = line_scatter_sum(by_block(attended_parts), "mp", count)
    layer_out = (inputs_float + attended).astype(jnp.bfloat16)

    grad_context = dot(cotangent, out_turned, NN).astype(jnp.bfloat16)
    grad_projected = attention_backward(projected, grad_context)
    normed_parts = dot(grad_projected, qkv_matrix, NT).astype(jnp.bfloat16)
    grad_normed = line_scatter_sum(by_block(normed_parts), "mp", count)

    out_term = dot(cotangent, context, TN).astype(jnp.bfloat16)
    out_sum = lax.psum_scatter(out_term, "dp", scatter_dimension=0, tiled=True)
    qkv_term = dot(normed, grad_projected, TN).astype(jnp.bfloat16)
    qkv_sum = lax.psum_scatter(
        qkv_term.reshape(width, 3, local_width), "dp", scatter_dimension=0, tiled=True
    )

    centre_grad = jnp.mean(grad_normed, axis=1, keepdims=True)
    along = jnp.mean(grad_normed * standard, axis=1, keepdims=True)
    grad_x = (
        upstream.astype(jnp.float32) + inv_scale * (grad_normed - centre_grad - standard * along)
    ).astype(jnp.bfloat16)
    return (layer_out, grad_x, qkv_sum.astype(jnp.bfloat16), out_sum.T.astype(jnp.bfloat16))


def solution(mesh):
    in_specs = (P(("dp", "mp"), None), P("dp", None, "mp"), P("mp", "dp"), P(("dp", "mp"), None))
    out_specs = (P(("dp", "mp"), None), P(("dp", "mp"), None), P("dp", None, "mp"), P("mp", "dp"))
    return jax.shard_map(
        functools.partial(per_device, mesh.shape["mp"]),
        mesh=mesh,
        in_specs=in_specs,
        out_specs=out_specs,
        check_vma=False,
    )
```

```python
import functools

import jax
import jax.numpy as jnp
from jax import lax
from jax.experimental import pallas as pl
from jax.experimental.pallas import tpu as pltpu
from jax.sharding import PartitionSpec as P

HD = 128
PATCH = 256
SCALE = HD ** (-0.5)
epsilon = 1e-06
VMEM_BYTES = 32 * 1024 * 1024

NT = (((1,), (1,)), ((), ()))
TN = (((0,), (0,)), ((), ()))
NN = (((1,), (0,)), ((), ()))


def dot(left, right, dims):
    return lax.dot_general(left, right, dims, preferred_element_type=jnp.float32)


def softmax_of(queries, keys):
    scores = dot(queries, keys, NT) * SCALE
    weights = jnp.exp(scores - jnp.max(scores, axis=-1, keepdims=True))
    return weights / jnp.sum(weights, axis=-1, keepdims=True)


def forward_kernel(projected_ref, context_ref):
    width = context_ref.shape[1]
    for low in range(0, width, HD):
        queries = projected_ref[:, low:low + HD]
        keys = projected_ref[:, width + low:width + low + HD]
        values = projected_ref[:, 2 * width + low:2 * width + low + HD]
        probs16 = softmax_of(queries, keys).astype(jnp.bfloat16)
        context_ref[:, low:low + HD] = dot(probs16, values, NN).astype(jnp.bfloat16)


def backward_kernel(projected_ref, grad_context_ref, grad_ref):
    width = grad_context_ref.shape[1]
    for low in range(0, width, HD):
        queries = projected_ref[:, low:low + HD]
        keys = projected_ref[:, width + low:width + low + HD]
        values = projected_ref[:, 2 * width + low:2 * width + low + HD]
        grad_heads = grad_context_ref[:, low:low + HD]
        probs = softmax_of(queries, keys)
        probs16 = probs.astype(jnp.bfloat16)
        grad_probs = dot(grad_heads, values, NT)
        row_totals = jnp.sum(probs * grad_probs, axis=-1, keepdims=True)
        grad_scores = (probs * (grad_probs - row_totals) * SCALE).astype(jnp.bfloat16)
        grad_ref[:, low:low + HD] = dot(grad_scores, keys, NN).astype(jnp.bfloat16)
        grad_ref[:, width + low:width + low + HD] = dot(grad_scores, queries, TN).astype(jnp.bfloat16)
        grad_ref[:, 2 * width + low:2 * width + low + HD] = dot(probs16, grad_heads, TN).astype(
            jnp.bfloat16
        )


def rows_spec(columns):
    return pl.BlockSpec((PATCH, columns), lambda image: (image, 0))


def attention_forward(projected):
    rows, width = projected.shape[0], projected.shape[1] // 3
    pairs = rows * width * PATCH // HD
    return pl.pallas_call(
        forward_kernel,
        grid=(rows // PATCH,),
        in_specs=[rows_spec(3 * width)],
        out_specs=rows_spec(width),
        out_shape=jax.ShapeDtypeStruct((rows, width), jnp.bfloat16),
        compiler_params=pltpu.CompilerParams(vmem_limit_bytes=VMEM_BYTES),
        cost_estimate=pl.CostEstimate(
            flops=4 * pairs * HD, bytes_accessed=8 * rows * width, transcendentals=pairs
        ),
        name="attention_forward",
    )(projected)


def attention_backward(projected, grad_context):
    rows, width = grad_context.shape
    pairs = rows * width * PATCH // HD
    return pl.pallas_call(
        backward_kernel,
        grid=(rows // PATCH,),
        in_specs=[rows_spec(3 * width), rows_spec(width)],
        out_specs=rows_spec(3 * width),
        out_shape=jax.ShapeDtypeStruct((rows, 3 * width), jnp.bfloat16),
        compiler_params=pltpu.CompilerParams(vmem_limit_bytes=VMEM_BYTES),
        cost_estimate=pl.CostEstimate(
            flops=10 * pairs * HD, bytes_accessed=14 * rows * width, transcendentals=pairs
        ),
        name="attention_backward",
    )(projected, grad_context)


def after(value, *others):
    return lax.optimization_barrier((value,) + others)[0]


def line_gather(block, axis, count, ties):
    me = lax.axis_index(axis)
    right, left = [block], [block]
    for step in range(1, count):
        rightward, leftward = right[-1], left[-1]
        if step in ties:
            rightward, leftward, _ = lax.optimization_barrier((rightward, leftward, ties[step]))
        right.append(
            lax.ppermute(rightward, axis, [(i, i + 1) for i in range(step - 1, count - 1)])
        )
        left.append(lax.ppermute(leftward, axis, [(i, i - 1) for i in range(1, count - step + 1)]))
    blocks = [block]
    for k in range(1, count):
        blocks.append(jnp.where(me >= k, right[k], left[count - k]))
    return blocks, (right[-1], left[-1])


def line_scatter_sum(parts, axis, count, ties):
    arrived = []
    for step in range(1, count):
        rightward, leftward = parts[step], parts[count - step]
        if step > 1:
            from_left, from_right = arrived[-1]
            rightward = (rightward.astype(jnp.float32) + from_left.astype(jnp.float32)).astype(
                jnp.bfloat16
            )
            leftward = (leftward.astype(jnp.float32) + from_right.astype(jnp.float32)).astype(
                jnp.bfloat16
            )
        if step in ties:
            rightward, leftward, _ = lax.optimization_barrier((rightward, leftward, ties[step]))
        arrived.append((
            lax.ppermute(rightward, axis, [(i, i + 1) for i in range(0, min(step, count - 1))]),
            lax.ppermute(leftward, axis, [(i, i - 1) for i in range(max(count - step, 1), count)]),
        ))
    total = parts[0].astype(jnp.float32)
    if arrived:
        total = total + arrived[-1][0].astype(jnp.float32) + arrived[-1][1].astype(jnp.float32)
    return total, arrived


def per_device(count, inputs, w_qkv, w_out, upstream):
    local_rows, width = inputs.shape
    local_width = w_qkv.shape[2]
    inputs_float = inputs.astype(jnp.float32)
    centred = inputs_float - jnp.mean(inputs_float, axis=1, keepdims=True)
    inv_scale = lax.rsqrt(jnp.mean(centred * centred, axis=1, keepdims=True) + epsilon)
    standard = centred * inv_scale
    normed_local = standard.astype(jnp.bfloat16)

    qkv_matrix = lax.all_gather(w_qkv, "dp", axis=0, tiled=True).reshape(width, 3 * local_width)
    out_cols = lax.all_gather(after(w_out, qkv_matrix), "dp", axis=1, tiled=True)

    def turned(blocks):
        if local_rows % PATCH == 0:
            return blocks
        stacked, me = jnp.stack(blocks), lax.axis_index("mp")
        return [
            lax.dynamic_index_in_dim(stacked, lax.rem(me + count - k, count), keepdims=False)
            for k in range(count)
        ]

    normed_blocks, last = line_gather(normed_local, "mp", count, {})
    normed = jnp.concatenate(turned(normed_blocks), axis=0)
    projected = dot(normed, qkv_matrix, NN).astype(jnp.bfloat16)
    context = attention_forward(projected)
    attended_parts = dot(context, out_cols, NN).astype(jnp.bfloat16)

    cotangent_blocks, _ = line_gather(
        upstream, "mp", count, {1: last, 2: projected, 3: attended_parts}
    )
    cotangent = jnp.concatenate(turned(cotangent_blocks), axis=0)

    def by_block(rows):
        return turned([rows[k * local_rows:(k + 1) * local_rows] for k in range(count)])

    attended, arrived = line_scatter_sum(by_block(attended_parts), "mp", count, {})
    layer_out = (inputs_float + attended).astype(jnp.bfloat16)

    cotangent = after(cotangent, *arrived[:1])
    grad_context = dot(cotangent, out_cols, NT).astype(jnp.bfloat16)
    grad_projected = after(attention_backward(projected, grad_context), *arrived[1:2])
    normed_parts = dot(grad_projected, qkv_matrix, NT).astype(jnp.bfloat16)
    grad_normed, _ = line_scatter_sum(by_block(normed_parts), "mp", count, {2: arrived})

    out_term = dot(cotangent, context, TN).astype(jnp.bfloat16)
    out_sum = lax.psum_scatter(out_term, "dp", scatter_dimension=0, tiled=True)
    grad_later = after(grad_projected, normed_parts)
    qkv_sums = []
    for low in range(0, 3 * local_width, local_width):
        term = dot(normed, grad_later[:, low:low + local_width], TN).astype(jnp.bfloat16)
        qkv_sums.append(lax.psum_scatter(term, "dp", scatter_dimension=0, tiled=True))
    qkv_sum = jnp.stack(qkv_sums, axis=1)

    centre_grad = jnp.mean(grad_normed, axis=1, keepdims=True)
    along = jnp.mean(grad_normed * standard, axis=1, keepdims=True)
    grad_x = (
        upstream.astype(jnp.float32) + inv_scale * (grad_normed - centre_grad - standard * along)
    ).astype(jnp.bfloat16)
    return (layer_out, grad_x, qkv_sum, out_sum.T)


def solution(mesh):
    in_specs = (P(("dp", "mp"), None), P("dp", None, "mp"), P("mp", "dp"), P(("dp", "mp"), None))
    out_specs = (P(("dp", "mp"), None), P(("dp", "mp"), None), P("dp", None, "mp"), P("mp", "dp"))
    return jax.shard_map(
        functools.partial(per_device, mesh.shape["mp"]),
        mesh=mesh,
        in_specs=in_specs,
        out_specs=out_specs,
        check_vma=False,
    )
```
